32 devices in a mesh: wide: 16 (over z, y, core), narrow: 2 (over x).
Axes of the slice: x: 2, y: 2, z: 4, core: 2. Of those that a mesh axis runs over, the one named last changes fastest.
Arguments:
- tile_values: bfloat16 [224, 512, 512], P(('wide', 'narrow')), may hold values from -0.25 to 0.25
- tile_row: int32 [224], P(('wide', 'narrow')), may hold values from 0 to 1
- tile_col: int32 [224], P(('wide', 'narrow')), may hold values from 0 to 1
- basis: float32 [32768, 256], P(('wide', 'narrow')), may hold values from -6 to 6
Outputs:
- next_basis: float32 [1024, 256], P('wide')
The draws below stay inside these ranges and needn't reach their ends.
All inputs are finite; a program needn't handle non-finite values.
Results may differ from the reference program's by a relative error of at most 0.0032.
Values sent between devices are 32-bit elements; how exact they have to be, the bound alone decides.
A program may use at most 64 MiB of HBM per device.

```python
import math
import jax
import jax.numpy as jnp
import numpy as np
from jax import lax

TILE = 512
RANK = 256
BLOCKS_DEV = 2
TILE_DEV = 7
COLS = 1024
COL_BLOCKS = 2
TILES = 224
ROWS = 32768


def set_ends(result, own_key, least, largest):
    place = [jax.random.randint(jax.random.fold_in(own_key, axis), (), 0, length) for axis, length in enumerate(result.shape)]
    main_axis = result.shape.index(max(result.shape))
    neighbour = place[:main_axis] + [(place[main_axis] + 1) % result.shape[main_axis]] + place[main_axis + 1:]
    return result.at[tuple(place)].set(least).at[tuple(neighbour)].set(largest)


def steps_of(own_key, dims, shards, low, high):
    loudness, own = 1.0, jax.random.fold_in(own_key, 6)
    for axis_at, shards_of in shards:
        heights = jnp.exp(jax.random.uniform(jax.random.fold_in(own, axis_at), (shards_of,), jnp.float32, low / len(shards), high / len(shards)))
        loudness = loudness * jnp.repeat(heights, dims[axis_at] // shards_of).reshape([-1 if axis == axis_at else 1 for axis in range(len(dims))])
    return loudness


def cumulative_ranks(amount, slope):
    loads = [(1 << 20) // math.isqrt(standing ** slope) + 1 for standing in range(1, amount + 1)]
    width = 1 + sum(loads) // (1 << 30)
    return np.cumsum(np.array([max(1, weight // width) for weight in loads]))


def ranked_ids(own_key, shape, count, lean):
    listing = cumulative_ranks(count, lean)
    ticket = jax.random.randint(jax.random.fold_in(own_key, 1), shape, 0, int(listing[count - 1]))
    standing = jnp.searchsorted(jnp.asarray(listing, jnp.int32), ticket, side="right")
    return jax.random.permutation(jax.random.fold_in(own_key, 2), count)[standing].astype(jnp.int32)


def scatter_about(own_key, dims, width, bound, pieces=(), held_as=jnp.bfloat16):
    values = jax.random.normal(own_key, dims, jnp.float32) * width
    if len(pieces) > 0:
        values = steps_of(own_key, dims, pieces, -0.22, 0.18) * values
    return jnp.clip(values, min=-bound, max=bound).astype(held_as)


def setup_inputs(seed: int = 0) -> dict:
    key_of = jax.random.split(jax.random.key(seed), 5)
    return {
        "tile_values": scatter_about(key_of[0], (TILES, TILE, TILE), TILE ** -0.5, 0.25, ((0, 32),)),
        "tile_row": set_ends(jax.random.randint(key_of[1], (TILES,), 0, BLOCKS_DEV), jax.random.fold_in(key_of[1], 1), 0, BLOCKS_DEV - 1).astype(jnp.int32),
        "tile_col": set_ends(ranked_ids(key_of[2], (TILES,), COL_BLOCKS, 3), jax.random.fold_in(key_of[2], 3), 0, COL_BLOCKS - 1).astype(jnp.int32),
        "basis": scatter_about(key_of[3], (ROWS, RANK), 1.0, 6.0, ((0, 32),), jnp.float32),
    }


def reference(tile_values, tile_row, tile_col, basis):
    devices = TILES // TILE_DEV
    rounded = basis.astype(jnp.bfloat16)
    rounded = lax.optimization_barrier(rounded).astype(jnp.float32)
    rounded = rounded.reshape(devices, BLOCKS_DEV, TILE, RANK)
    tile_groups = tile_values.reshape(devices, TILE_DEV, TILE, TILE)
    row_groups = tile_row.reshape(devices, TILE_DEV)
    col_groups = tile_col.reshape(devices, TILE_DEV)

    def accumulate(running, inputs):
        group_tiles, group_rows, group_cols, blocks = inputs
        chosen = jnp.take(blocks, group_rows, axis=0)
        products = jnp.einsum('tij,tik->tjk', group_tiles.astype(jnp.float32), chosen, precision=lax.Precision.HIGHEST)
        one_hot = (group_cols[None, :] == jnp.arange(COL_BLOCKS, dtype=jnp.int32)[:, None]).astype(jnp.float32)
        return (running + jnp.einsum('ct,tjk->cjk', one_hot, products, precision=lax.Precision.HIGHEST), None)
    start = jnp.zeros((COL_BLOCKS, TILE, RANK), jnp.float32)
    summed, _ = lax.scan(accumulate, start, (tile_groups, row_groups, col_groups, rounded))
    gathered = summed.reshape(COLS, RANK)
    gram_sum = jnp.dot(gathered.T.astype(jnp.float32), gathered.astype(jnp.float32), precision=lax.Precision.HIGHEST, preferred_element_type=jnp.float32) / COLS
    factor = jnp.linalg.cholesky(gram_sum)
    return jax.scipy.linalg.solve_triangular(factor, gathered.T, lower=True).T
```

```python
import functools

import jax
import jax.numpy as jnp
from jax import lax
from jax.experimental import pallas as pl
from jax.experimental.pallas import tpu as pltpu
from jax.sharding import PartitionSpec as P

MESH = pl.DeviceIdType.MESH
HIGHEST = lax.Precision.HIGHEST
VMEM_LIMIT = 48 * 1024 * 1024
COLS_DEV = 64


def local_kernel(row_ref, col_ref, tile_ref, basis_ref, out_ref, rounded):
    t = pl.program_id(0)
    edge = tile_ref.shape[1]

    @pl.when(t == 0)
    def _():
        rounded[...] = basis_ref[...].astype(jnp.bfloat16)
        out_ref[...] = jnp.zeros_like(out_ref)

    r = pl.multiple_of(row_ref[t] * edge, edge)
    c = pl.multiple_of(col_ref[t] * edge, edge)
    out_ref[pl.ds(c, edge), :] += lax.dot_general(
        tile_ref[0],
        rounded[pl.ds(r, edge), :],
        (((0,), (0,)), ((), ())),
        preferred_element_type=jnp.float32,
    )


def local_terms(tile_values, tile_row, tile_col, basis, total_rows):
    tiles, edge, _ = tile_values.shape
    rows, rank = basis.shape
    return pl.pallas_call(
        local_kernel,
        out_shape=jax.ShapeDtypeStruct((total_rows, rank), jnp.float32),
        grid_spec=pltpu.PrefetchScalarGridSpec(
            num_scalar_prefetch=2,
            grid=(tiles,),
            in_specs=[
                pl.BlockSpec((1, edge, edge), lambda t, *_: (t, 0, 0)),
                pl.BlockSpec((rows, rank), lambda t, *_: (0, 0)),
            ],
            out_specs=pl.BlockSpec((total_rows, rank), lambda t, *_: (0, 0)),
            scratch_shapes=[pltpu.VMEM((rows, rank), jnp.bfloat16)],
        ),
        compiler_params=pltpu.CompilerParams(vmem_limit_bytes=VMEM_LIMIT),
    )(tile_row, tile_col, tile_values, basis)


def stream_orders(n_wide, n_narrow, chunk_rows):
    nb = n_narrow.bit_length() - 1
    wb = n_wide.bit_length() - 1
    core = [nb]
    narrow = list(range(nb))
    rest = [nb + i for i in range(1, wb)]
    first = core + narrow + rest
    second = core + rest[:1] + narrow + rest[1:]
    return [first, second] if chunk_rows % 16 == 0 else [first]


def split_sizes(order, step):
    left = sorted(order[step:])
    at = left.index(order[step])
    return 2 ** (len(left) - 1 - at), 2**at


def sum_gather_kernel(n_narrow, orders, part_ref, *refs):
    out_refs = refs[: len(orders)]
    recv0, recvs, accs, send_sem, recv_sem, gsend_sem, grecv_sem = refs[len(orders) :]
    w, n = lax.axis_index("wide"), lax.axis_index("narrow")
    me = w * n_narrow + n
    steps = len(orders[0])
    streams = len(orders)
    rows = out_refs[0].shape[1]

    def bit(b):
        return (me // (2**b)) % 2

    def partner(b):
        other = me + (1 - 2 * bit(b)) * (2**b)
        return (other // n_narrow, other % n_narrow)

    barrier = pltpu.get_barrier_semaphore()
    for b in range(steps):
        pl.semaphore_signal(barrier, inc=1, device_id=partner(b), device_id_type=MESH)
    pl.semaphore_wait(barrier, steps)

    b = orders[0][0]
    mine = bit(b)
    copy = pltpu.make_async_remote_copy(
        src_ref=part_ref.at[:, 1 - mine],
        dst_ref=recv0,
        send_sem=send_sem.at[0, 0],
        recv_sem=recv_sem.at[0, 0],
        device_id=partner(b),
        device_id_type=MESH,
    )
    copy.start()
    copy.wait()
    for s in range(streams):
        lanes = pl.ds(s * rows, rows)
        both = part_ref[:, pl.ds(mine, 1), :, lanes][:, 0] + recv0[:, :, lanes]
        accs[s][0][...] = both.reshape(accs[s][0].shape)

    copies = [None] * streams
    for step in range(1, steps):
        for s in range(streams):
            b = orders[s][step]
            copies[s] = pltpu.make_async_remote_copy(
                src_ref=accs[s][step - 1].at[:, 1 - bit(b)],
                dst_ref=recvs[s][step - 1],
                send_sem=send_sem.at[step, s],
                recv_sem=recv_sem.at[step, s],
                device_id=partner(b),
                device_id_type=MESH,
            )
            copies[s].start()
        for s in range(streams):
            mine = bit(orders[s][step])
            copies[s].wait()
            both = accs[s][step - 1][:, pl.ds(mine, 1)][:, 0] + recvs[s][step - 1][...]
            if step < steps - 1:
                accs[s][step][...] = both.reshape(accs[s][step].shape)
            else:
                place = place_of(orders[s], w, n, n_narrow)
                out_refs[s][pl.ds(place, 1)] = both.reshape((1,) + out_refs[s].shape[1:])

    for i in range(steps):
        for s in range(streams):
            b = orders[s][steps - 1 - i]
            place = place_of(orders[s], w, n, n_narrow)
            size = 2**i
            block = out_refs[s].at[pl.ds((place // size) * size, size)]
            copies[s] = pltpu.make_async_remote_copy(
                src_ref=block,
                dst_ref=block,
                send_sem=gsend_sem.at[i, s],
                recv_sem=grecv_sem.at[i, s],
                device_id=partner(b),
                device_id_type=MESH,
            )
            copies[s].start()
        for s in range(streams):
            copies[s].wait()


def place_of(order, w, n, n_narrow):
    number = w * n_narrow + n
    place = 0
    for i, b in enumerate(reversed(order)):
        place = place + ((number // (2**b)) % 2) * (2**i)
    return place


def sum_and_gather(partial, n_wide, n_narrow):
    total_rows, rank = partial.shape
    devices = n_wide * n_narrow
    chunk = total_rows // devices
    orders = stream_orders(n_wide, n_narrow, chunk)
    steps, streams = len(orders[0]), len(orders)
    rows = chunk // streams
    hi, lo = split_sizes(orders[0], 0)
    recvs, accs = [], []
    for order in orders:
        recv, acc = [], []
        for step in range(1, steps):
            up, down = split_sizes(order, step)
            acc.append(pltpu.VMEM((up, 2, down, rows, rank), jnp.float32))
            recv.append(pltpu.VMEM((up, down, rows, rank), jnp.float32))
        recvs.append(recv)
        accs.append(acc)
    block = pl.BlockSpec(memory_space=pltpu.VMEM)
    sems = pltpu.SemaphoreType.DMA((steps, streams))
    return pl.pallas_call(
        functools.partial(sum_gather_kernel, n_narrow, orders),
        out_shape=[jax.ShapeDtypeStruct((devices, rows, rank), jnp.float32)] * streams,
        in_specs=[block],
        out_specs=[block] * streams,
        scratch_shapes=[pltpu.VMEM((hi, lo, chunk, rank), jnp.float32), recvs, accs, sems, sems, sems, sems],
        compiler_params=pltpu.CompilerParams(collective_id=0, has_side_effects=True, vmem_limit_bytes=VMEM_LIMIT),
    )(partial.reshape(hi, 2, lo, chunk, rank)), orders


LANES = 128
PANEL = 8
OUTER = 32


def splat(value):
    return jnp.broadcast_to(value, (PANEL, LANES))


def finish_kernel(orders, n_narrow, *refs):
    streams = len(orders)
    y_refs, out_ref, work = refs[:streams], refs[streams], refs[streams + 1]
    devices, rows, rank = y_refs[0].shape
    owned = out_ref.shape[0]
    total_rows = devices * rows * streams
    width = work.shape[1]
    w = lax.axis_index("wide")

    gram = jnp.zeros((rank, rank), jnp.float32)
    for s in range(streams):
        flat = y_refs[s][...].reshape(devices * rows, rank)
        gram += lax.dot_general(
            flat, flat, (((0,), (0,)), ((), ())), precision=HIGHEST, preferred_element_type=jnp.float32
        )
    work[:, :rank] = gram * (1.0 / total_rows)
    pieces = []
    for n in range(n_narrow):
        for s in range(streams):
            pieces.append(y_refs[s][place_of(orders[s], w, n, n_narrow)])
    pieces.append(jnp.zeros((width - rank - owned, rank), jnp.float32))
    work[:, rank:] = jnp.concatenate(pieces, axis=0).T

    for outer in range(0, rank, OUTER):
        base = (outer // LANES) * LANES
        blocks = list(range(base, width, LANES))
        groups = [
            [work[outer + g : outer + g + PANEL, c : c + LANES] for c in blocks] for g in range(0, OUTER, PANEL)
        ]
        for p in range(OUTER // PANEL):
            k = outer + p * PANEL - base
            head = groups[p][0]
            cols = [splat(head[:, k + j : k + j + 1]) for j in range(PANEL)]
            entry = [[splat(cols[j][i : i + 1, :]) for j in range(i + 1)] for i in range(PANEL)]
            scale = []
            for j in range(PANEL):
                scale.append(lax.rsqrt(entry[j][j]))
                for i in range(j + 1, PANEL):
                    entry[i][j] = entry[i][j] * scale[j]
                for i in range(j + 1, PANEL):
                    for m in range(j + 1, i + 1):
                        entry[i][m] = entry[i][m] - entry[i][j] * entry[m][j]
            solved = [[splat(block[j : j + 1, :]) for block in groups[p]] for j in range(PANEL)]
            for j in range(PANEL):
                solved[j] = [v * scale[j] for v in solved[j]]
                for i in range(j + 1, PANEL):
                    solved[i] = [a - entry[i][j] * v for a, v in zip(solved[i], solved[j])]
            place = lax.broadcasted_iota(jnp.int32, (PANEL, LANES), 0)
            final = solved[0]
            for j in range(1, PANEL):
                final = [jnp.where(place == j, v, f) for v, f in zip(solved[j], final)]
            for g in range(p + 1, OUTER // PANEL):
                low = groups[g][0]
                mult = [splat(low[:, k + j : k + j + 1]) for j in range(PANEL)]
                for j in range(PANEL):
                    mult[j] = mult[j] * scale[j]
                    for i in range(j + 1, PANEL):
                        mult[i] = mult[i] - entry[i][j] * mult[j]
                for j in range(PANEL):
                    groups[g] = [a - mult[j] * v for a, v in zip(groups[g], solved[j])]
            row = outer + p * PANEL
            for c, f in zip(blocks, final):
                work[row : row + PANEL, c : c + LANES] = f
        after = outer + OUTER
        if after < rank:
            start = (after // LANES) * LANES
            done = work[outer:after, start:]
            update = lax.dot_general(
                done[:, after - start : rank - start],
                done,
                (((0,), (0,)), ((), ())),
                precision=HIGHEST,
                preferred_element_type=jnp.float32,
            )
            work[after:rank, start:] -= update
    out_ref[...] = work[:, rank:].T[:owned]


def finish(gathered, orders, owned, n_narrow):
    rank = gathered[0].shape[-1]
    width = rank + -(-owned // LANES) * LANES
    return pl.pallas_call(
        functools.partial(finish_kernel, orders, n_narrow),
        out_shape=jax.ShapeDtypeStruct((owned, rank), jnp.float32),
        in_specs=[pl.BlockSpec(memory_space=pltpu.VMEM)] * len(gathered),
        out_specs=pl.BlockSpec(memory_space=pltpu.VMEM),
        scratch_shapes=[pltpu.VMEM((rank, width), jnp.float32)],
        compiler_params=pltpu.CompilerParams(vmem_limit_bytes=VMEM_LIMIT),
    )(*gathered)


def solution(mesh):
    n_wide, n_narrow = mesh.shape["wide"], mesh.shape["narrow"]
    owned = COLS_DEV

    def body(tile_values, tile_row, tile_col, basis):
        total_rows = owned * n_wide
        partial = local_terms(tile_values, tile_row, tile_col, basis, total_rows)
        gathered, orders = sum_and_gather(partial, n_wide, n_narrow)
        return finish(gathered, orders, owned, n_narrow)

    in_specs = (
        P(("wide", "narrow"), None, None),
        P(("wide", "narrow")),
        P(("wide", "narrow")),
        P(("wide", "narrow"), None),
    )
    return jax.shard_map(body, mesh=mesh, in_specs=in_specs, out_specs=P("wide", None), check_vma=False)
```

```python
import functools

import jax
import jax.numpy as jnp
from jax import lax
from jax.experimental import pallas as pl
from jax.experimental.pallas import tpu as pltpu
from jax.sharding import PartitionSpec as P

MESH = pl.DeviceIdType.MESH
HIGHEST = lax.Precision.HIGHEST
VMEM_LIMIT = 48 * 1024 * 1024
COLS_DEV = 64
LANES = 128


def local_kernel(row_hbm, col_hbm, tile_hbm, basis_hbm, out_ref, row_ref, col_ref, tiles, basis, rounded, sem, tile_sem):
    count, edge, _ = tiles.shape
    small = [
        pltpu.make_async_copy(row_hbm, row_ref, sem.at[0]),
        pltpu.make_async_copy(col_hbm, col_ref, sem.at[1]),
        pltpu.make_async_copy(basis_hbm, basis, sem.at[2]),
    ]
    large = [pltpu.make_async_copy(tile_hbm.at[t], tiles.at[t], tile_sem.at[t]) for t in range(count)]
    for copy in small + large:
        copy.start()
    out_ref[...] = jnp.zeros_like(out_ref)
    for copy in small:
        copy.wait()
    rounded[...] = basis[...].astype(jnp.bfloat16)
    for t in range(count):
        large[t].wait()
        r = pl.multiple_of(row_ref[t] * edge, edge)
        c = pl.multiple_of(col_ref[t] * edge, edge)
        out_ref[pl.ds(c, edge), :] += lax.dot_general(
            tiles[t],
            rounded[pl.ds(r, edge), :],
            (((0,), (0,)), ((), ())),
            preferred_element_type=jnp.float32,
        )


def local_terms(tile_values, tile_row, tile_col, basis, total_rows):
    count = tile_values.shape[0]
    rows, rank = basis.shape
    return pl.pallas_call(
        local_kernel,
        out_shape=jax.ShapeDtypeStruct((total_rows, rank), jnp.float32),
        in_specs=[pl.BlockSpec(memory_space=pltpu.HBM)] * 4,
        out_specs=pl.BlockSpec(memory_space=pltpu.VMEM),
        scratch_shapes=[
            pltpu.SMEM((count,), jnp.int32),
            pltpu.SMEM((count,), jnp.int32),
            pltpu.VMEM(tile_values.shape, jnp.bfloat16),
            pltpu.VMEM((rows, rank), jnp.float32),
            pltpu.VMEM((rows, rank), jnp.bfloat16),
            pltpu.SemaphoreType.DMA((3,)),
            pltpu.SemaphoreType.DMA((count,)),
        ],
        compiler_params=pltpu.CompilerParams(vmem_limit_bytes=VMEM_LIMIT),
    )(tile_row, tile_col, tile_values, basis)


def stream_orders(n_wide, n_narrow, chunk_rows):
    nb = n_narrow.bit_length() - 1
    wb = n_wide.bit_length() - 1
    core = [(nb,)]
    narrow = [(i,) for i in range(nb)]
    second = [(nb + i,) for i in range(1, min(wb, 2))]
    rest = [tuple(range(nb + i, min(nb + i + 2, nb + wb))) for i in range(2, wb, 2)]
    pair = [core + narrow + second + rest, core + second + narrow + rest]
    if chunk_rows % 32 == 0:
        return pair + pair
    return pair if chunk_rows % 16 == 0 else pair[:1]


def split_sizes(order, step):
    left = sorted(b for group in order[step:] for b in group)
    at = left.index(order[step][0])
    size = len(order[step])
    return 2 ** (len(left) - at - size), 2**size, 2**at


def place_of(order, number):
    place, scale = 0, 1
    for group in reversed(order[1:]):
        place = place + ((number // 2 ** group[0]) % 2 ** len(group)) * scale
        scale = scale * 2 ** len(group)
    return place


def sum_gather_kernel(n_narrow, orders, part_ref, gram_ref, owned_ref, recvs, accs, rows_all, gram_own, gram_in, sems):
    w, n = lax.axis_index("wide"), lax.axis_index("narrow")
    me = w * n_narrow + n
    steps, streams = len(orders[0]), len(orders)
    rows, rank = rows_all.shape[2], rows_all.shape[3]
    send_sem, recv_sem, gather_send, gather_recv, gram_send, gram_recv = sems

    def partner(group, delta):
        other, digit = me, (me // 2 ** group[0]) % 2 ** len(group)
        for i, b in enumerate(group):
            if (delta >> i) & 1:
                turn = 1 - 2 * ((me // 2**b) % 2)
                other, digit = other + turn * 2**b, digit + turn * 2**i
        return {"wide": other // n_narrow, "narrow": other % n_narrow}, digit

    barrier = pltpu.get_barrier_semaphore()
    met = 0
    for group in orders[0]:
        for delta in range(1, 2 ** len(group)):
            device, _ = partner(group, delta)
            pl.semaphore_signal(barrier, inc=1, device_id=device, device_id_type=MESH)
            met += 1
    pl.semaphore_wait(barrier, met)

    def block_of(step, s, digit):
        if step == 0:
            return part_ref.at[:, digit, :, pl.ds(s * rows, rows)]
        return accs[s][step - 1].at[:, digit]

    def start_sum(step, s):
        group, copies = orders[s][step], []
        for delta in range(1, 2 ** len(group)):
            device, digit = partner(group, delta)
            copy = pltpu.make_async_remote_copy(
                src_ref=block_of(step, s, digit),
                dst_ref=recvs[s][step].at[delta - 1],
                send_sem=send_sem.at[step, s, delta - 1],
                recv_sem=recv_sem.at[step, s, delta - 1],
                device_id=device,
                device_id_type=MESH,
            )
            copy.start()
            copies.append(copy)
        return copies

    def start_gather(step, s):
        group, copies = orders[s][step], []
        size = 1
        for later in orders[s][step + 1 :]:
            size = size * 2 ** len(later)
        place = place_of(orders[s], me)
        block = rows_all.at[s, pl.ds((place // size) * size, size)]
        for delta in range(1, 2 ** len(group)):
            device, _ = partner(group, delta)
            copy = pltpu.make_async_remote_copy(
                src_ref=block,
                dst_ref=block,
                send_sem=gather_send.at[step, s, delta - 1],
                recv_sem=gather_recv.at[step, s, delta - 1],
                device_id=device,
                device_id_type=MESH,
            )
            copy.start()
            copies.append(copy)
        return copies

    flying = [start_sum(0, s) for s in range(streams)]
    for step in range(steps):
        for s in range(streams):
            group = orders[s][step]
            digit = (me // 2 ** group[0]) % 2 ** len(group)
            total = block_of(step, s, digit)[...]
            for delta, copy in enumerate(flying[s]):
                copy.wait()
                total = total + recvs[s][step][delta]
            if step < steps - 1:
                accs[s][step][...] = total.reshape(accs[s][step].shape)
                flying[s] = start_sum(step + 1, s)
            else:
                rows_all[s, pl.ds(place_of(orders[s], me), 1)] = total.reshape((1, rows, rank))
                flying[s] = start_gather(step, s)
    for step in range(steps - 1, 0, -1):
        for s in range(streams):
            for copy in flying[s]:
                copy.wait()
            if step > 1:
                flying[s] = start_gather(step - 1, s)

    held = rows_all[...].reshape(-1, rank)
    device, _ = partner(orders[0][0], 1)
    copies = []
    for i, at in enumerate(range(0, rank, LANES)):
        place = (slice(at, at + LANES), slice(at, rank))
        gram_own[place] = lax.dot_general(
            held[:, at : at + LANES],
            held[:, at:],
            (((0,), (0,)), ((), ())),
            precision=HIGHEST,
            preferred_element_type=jnp.float32,
        )
        copy = pltpu.make_async_remote_copy(
            src_ref=gram_own.at[pl.ds(at, LANES), pl.ds(at, rank - at)],
            dst_ref=gram_in.at[pl.ds(at, LANES), pl.ds(at, rank - at)],
            send_sem=gram_send.at[i],
            recv_sem=gram_recv.at[i],
            device_id=device,
            device_id_type=MESH,
        )
        copy.start()
        copies.append(copy)
    for other in range(n_narrow):
        for s in range(streams):
            at = (other * streams + s) * rows
            owned_ref[at : at + rows, :] = rows_all[s, place_of(orders[s], w * n_narrow + other)]
    for at, copy in zip(range(0, rank, LANES), copies):
        copy.wait()
        place = (slice(at, at + LANES), slice(at, rank))
        gram_ref[place] = gram_own[place] + gram_in[place]
        if at > 0:
            gram_ref[at : at + LANES, :at] = jnp.zeros((LANES, at), jnp.float32)


def sum_and_gather(partial, n_wide, n_narrow):
    total_rows, rank = partial.shape
    devices = n_wide * n_narrow
    chunk = total_rows // devices
    orders = stream_orders(n_wide, n_narrow, chunk)
    steps, streams = len(orders[0]), len(orders)
    rows = chunk // streams
    recvs, accs = [], []
    for order in orders:
        recv, acc = [], []
        for step in range(steps):
            up, size, down = split_sizes(order, step)
            recv.append(pltpu.VMEM((size - 1, up, down, rows, rank), jnp.float32))
            if step > 0:
                acc.append(pltpu.VMEM((up, size, down, rows, rank), jnp.float32))
        recvs.append(recv)
        accs.append(acc)
    up, size, down = split_sizes(orders[0], 0)
    block = pl.BlockSpec(memory_space=pltpu.VMEM)
    most = max(2 ** len(group) for group in orders[0]) - 1
    sems = [pltpu.SemaphoreType.DMA((steps, streams, most))] * 4 + [pltpu.SemaphoreType.DMA((rank // LANES,))] * 2
    square = pltpu.VMEM((rank, rank), jnp.float32)
    return pl.pallas_call(
        functools.partial(sum_gather_kernel, n_narrow, orders),
        out_shape=[
            jax.ShapeDtypeStruct((rank, rank), jnp.float32),
            jax.ShapeDtypeStruct((chunk * n_narrow, rank), jnp.float32),
        ],
        in_specs=[block],
        out_specs=[block] * 2,
        scratch_shapes=[
            recvs,
            accs,
            pltpu.VMEM((streams, devices // 2, rows, rank), jnp.float32),
            square,
            square,
            sems,
        ],
        compiler_params=pltpu.CompilerParams(collective_id=0, has_side_effects=True, vmem_limit_bytes=VMEM_LIMIT),
    )(partial.reshape(up, size, down, chunk, rank))


PANEL = 8
OUTER = 32


def splat(value):
    return jnp.broadcast_to(value, (PANEL, LANES))


def finish_kernel(total_rows, gram_ref, owned_ref, out_ref, work):
    owned, rank = owned_ref.shape
    width = work.shape[1]
    work[:, :rank] = gram_ref[...] * (1.0 / total_rows)
    filled = jnp.concatenate([owned_ref[...], jnp.zeros((width - rank - owned, rank), jnp.float32)], axis=0)
    work[:, rank:] = filled.T

    for outer in range(0, rank, OUTER):
        base = (outer // LANES) * LANES
        blocks = list(range(base, width, LANES))
        groups = [
            [work[outer + g : outer + g + PANEL, c : c + LANES] for c in blocks] for g in range(0, OUTER, PANEL)
        ]
        for p in range(OUTER // PANEL):
            k = outer + p * PANEL - base
            head = groups[p][0]
            cols = [splat(head[:, k + j : k + j + 1]) for j in range(PANEL)]
            entry = [[splat(cols[j][i : i + 1, :]) for j in range(i + 1)] for i in range(PANEL)]
            scale = []
            for j in range(PANEL):
                scale.append(lax.rsqrt(entry[j][j]))
                for i in range(j + 1, PANEL):
                    entry[i][j] = entry[i][j] * scale[j]
                for i in range(j + 1, PANEL):
                    for m in range(j + 1, i + 1):
                        entry[i][m] = entry[i][m] - entry[i][j] * entry[m][j]
            solved = [[splat(block[j : j + 1, :]) for block in groups[p]] for j in range(PANEL)]
            for j in range(PANEL):
                solved[j] = [v * scale[j] for v in solved[j]]
                for i in range(j + 1, PANEL):
                    solved[i] = [a - entry[i][j] * v for a, v in zip(solved[i], solved[j])]
            place = lax.broadcasted_iota(jnp.int32, (PANEL, LANES), 0)
            final = solved[0]
            for j in range(1, PANEL):
                final = [jnp.where(place == j, v, f) for v, f in zip(solved[j], final)]
            for g in range(p + 1, OUTER // PANEL):
                low = groups[g][0]
                mult = [splat(low[:, k + j : k + j + 1]) for j in range(PANEL)]
                for j in range(PANEL):
                    mult[j] = mult[j] * scale[j]
                    for i in range(j + 1, PANEL):
                        mult[i] = mult[i] - entry[i][j] * mult[j]
                for j in range(PANEL):
                    groups[g] = [a - mult[j] * v for a, v in zip(groups[g], solved[j])]
            row = outer + p * PANEL
            for c, f in zip(blocks, final):
                work[row : row + PANEL, c : c + LANES] = f
        after = outer + OUTER
        if after < rank:
            start = (after // LANES) * LANES
            done = work[outer:after, start:]
            update = lax.dot_general(
                done[:, after - start : rank - start],
                done,
                (((0,), (0,)), ((), ())),
                precision=HIGHEST,
                preferred_element_type=jnp.float32,
            )
            work[after:rank, start:] -= update
    out_ref[...] = work[:, rank:].T[:owned]


def finish(gram, owned_rows, total_rows):
    owned, rank = owned_rows.shape
    width = rank + -(-owned // LANES) * LANES
    block = pl.BlockSpec(memory_space=pltpu.VMEM)
    return pl.pallas_call(
        functools.partial(finish_kernel, total_rows),
        out_shape=jax.ShapeDtypeStruct((owned, rank), jnp.float32),
        in_specs=[block] * 2,
        out_specs=block,
        scratch_shapes=[pltpu.VMEM((rank, width), jnp.float32)],
        compiler_params=pltpu.CompilerParams(vmem_limit_bytes=VMEM_LIMIT),
    )(gram, owned_rows)


def solution(mesh):
    n_wide, n_narrow = mesh.shape["wide"], mesh.shape["narrow"]
    owned = COLS_DEV

    def body(tile_values, tile_row, tile_col, basis):
        total_rows = owned * n_wide
        partial = local_terms(tile_values, tile_row, tile_col, basis, total_rows)
        gram, owned_rows = sum_and_gather(partial, n_wide, n_narrow)
        return finish(gram, owned_rows, total_rows)

    in_specs = (
        P(("wide", "narrow"), None, None),
        P(("wide", "narrow")),
        P(("wide", "narrow")),
        P(("wide", "narrow"), None),
    )
    return jax.shard_map(body, mesh=mesh, in_specs=in_specs, out_specs=P("wide", None), check_vma=False)
```

```python
import functools

import jax
import jax.numpy as jnp
from jax import lax
from jax.experimental import pallas as pl
from jax.experimental.pallas import tpu as pltpu
from jax.sharding import PartitionSpec as P

MESH = pl.DeviceIdType.MESH
HIGHEST = lax.Precision.HIGHEST
VMEM_LIMIT = 62 * 1024 * 1024
FINISH_LIMIT = 62 * 1024 * 1024
HALVES = 2
COLS_DEV = 64
LANES = 128


def stream_orders(n_wide, n_narrow, chunk_rows):
    nb = n_narrow.bit_length() - 1
    wb = n_wide.bit_length() - 1
    core = [(nb,)]
    narrow = [(i,) for i in range(nb)]
    second = [(nb + i,) for i in range(1, min(wb, 2))]
    rest = [tuple(range(nb + i, min(nb + i + 2, nb + wb))) for i in range(2, wb, 2)]
    pair = [core + narrow + second + rest, core + second + narrow + rest]
    if chunk_rows % 32 == 0:
        return pair + pair
    return pair if chunk_rows % 16 == 0 else pair[:1]


def split_sizes(order, step):
    left = sorted(b for group in order[step:] for b in group)
    at = left.index(order[step][0])
    size = len(order[step])
    return 2 ** (len(left) - at - size), 2**size, 2**at


def place_of(order, number):
    place, scale = 0, 1
    for group in reversed(order[1:]):
        place = place + ((number // 2 ** group[0]) % 2 ** len(group)) * scale
        scale = scale * 2 ** len(group)
    return place


def sum_gather_kernel(n_narrow, orders, row_ref, col_ref, tile_hbm, basis_hbm, gram_ref, owned_ref, *scratch):
    tiles, basis, rounded, part, recv0, recvs, accs, rows_all, gram_own, gram_in, sems = scratch
    w, n = lax.axis_index("wide"), lax.axis_index("narrow")
    me = w * n_narrow + n
    steps, streams = len(orders[0]), len(orders)
    rows, rank = rows_all.shape[2], rows_all.shape[3]
    basis_sem, tile_sem, core_send, core_recv, send_sem, recv_sem, gather_send, gather_recv, gram_send, gram_recv = sems
    count, edge, strip = tiles.shape[1:]

    def partner(group, delta):
        other, digit = me, (me // 2 ** group[0]) % 2 ** len(group)
        for i, b in enumerate(group):
            if (delta >> i) & 1:
                turn = 1 - 2 * ((me // 2**b) % 2)
                other, digit = other + turn * 2**b, digit + turn * 2**i
        return {"wide": other // n_narrow, "narrow": other % n_narrow}, digit

    barrier = pltpu.get_barrier_semaphore()
    met = 0
    for group in orders[0]:
        for delta in range(1, 2 ** len(group)):
            device, _ = partner(group, delta)
            pl.semaphore_signal(barrier, inc=1, device_id=device, device_id_type=MESH)
            met += 1

    def block_of(step, s, digit):
        if step == 0:
            return part.at[:, :, :, digit, :, pl.ds(s * rows, rows)]
        return accs[s][step - 1].at[:, digit]

    def start_sum(step, s):
        group, copies = orders[s][step], []
        for delta in range(1, 2 ** len(group)):
            device, digit = partner(group, delta)
            copy = pltpu.make_async_remote_copy(
                src_ref=block_of(step, s, digit),
                dst_ref=recvs[s][step - 1].at[delta - 1],
                send_sem=send_sem.at[step, s, delta - 1],
                recv_sem=recv_sem.at[step, s, delta - 1],
                device_id=device,
                device_id_type=MESH,
            )
            copy.start()
            copies.append(copy)
        return copies

    def start_gather(step, s):
        group, copies = orders[s][step], []
        size = 1
        for later in orders[s][step + 1 :]:
            size = size * 2 ** len(later)
        place = place_of(orders[s], me)
        block = rows_all.at[s, pl.ds((place // size) * size, size)]
        for delta in range(1, 2 ** len(group)):
            device, _ = partner(group, delta)
            copy = pltpu.make_async_remote_copy(
                src_ref=block,
                dst_ref=block,
                send_sem=gather_send.at[step, s, delta - 1],
                recv_sem=gather_recv.at[step, s, delta - 1],
                device_id=device,
                device_id_type=MESH,
            )
            copy.start()
            copies.append(copy)
        return copies

    copies = [pltpu.make_async_copy(basis_hbm, basis, basis_sem.at[0])]
    for h in range(HALVES):
        for t in range(count):
            source = tile_hbm.at[t, :, pl.ds(h * strip, strip)]
            copies.append(pltpu.make_async_copy(source, tiles.at[h, t], tile_sem.at[h, t]))
    for copy in copies:
        copy.start()
    copies[0].wait()
    rounded[...] = basis[...].astype(jnp.bfloat16).reshape(rounded.shape)
    core, other = (me // 2 ** orders[0][0][0]) % 2, partner(orders[0][0], 1)
    core_copies = []
    for h in range(HALVES):
        for t in range(count):
            copies[1 + h * count + t].wait()
            product = lax.dot_general(
                tiles[h, t], rounded[row_ref[t]], (((0,), (0,)), ((), ())), preferred_element_type=jnp.float32
            ).reshape(part.shape[2:])
            for c in range(part.shape[0]):
                term = jnp.where(col_ref[t] == c, product, 0.0)
                part[c, h] = term if t == 0 else part[c, h] + term
        if h == 0:
            pl.semaphore_wait(barrier, met)
        for c in range(part.shape[0]):
            copy = pltpu.make_async_remote_copy(
                src_ref=part.at[c, h, :, other[1]],
                dst_ref=recv0.at[c, h],
                send_sem=core_send.at[c, h],
                recv_sem=core_recv.at[c, h],
                device_id=other[0],
                device_id_type=MESH,
            )
            copy.start()
            core_copies.append(copy)
    for copy in core_copies:
        copy.wait()
    flying = []
    for s in range(streams):
        total = block_of(0, s, core)[...] + recv0[:, :, :, :, s * rows : (s + 1) * rows]
        accs[s][0][...] = total.reshape(accs[s][0].shape)
        flying.append(start_sum(1, s))

    for step in range(1, steps):
        for s in range(streams):
            group = orders[s][step]
            digit = (me // 2 ** group[0]) % 2 ** len(group)
            total = block_of(step, s, digit)[...]
            for delta, copy in enumerate(flying[s]):
                copy.wait()
                total = total + recvs[s][step - 1][delta]
            if step < steps - 1:
                accs[s][step][...] = total.reshape(accs[s][step].shape)
                flying[s] = start_sum(step + 1, s)
            else:
                rows_all[s, pl.ds(place_of(orders[s], me), 1)] = total.reshape((1, rows, rank))
                flying[s] = start_gather(step, s)
    for step in range(steps - 1, 1, -1):
        for s in range(streams):
            for copy in flying[s]:
                copy.wait()
            flying[s] = start_gather(step - 1, s)

    def gram_block(held, at):
        return lax.dot_general(
            held[:, at : at + LANES],
            held[:, at:],
            (((0,), (0,)), ((), ())),
            precision=HIGHEST,
            preferred_element_type=jnp.float32,
        )

    early = streams // 2
    for s in range(early):
        for copy in flying[s]:
            copy.wait()
    if early:
        held = rows_all[:early].reshape(-1, rank)
        for at in range(0, rank, LANES):
            gram_own[at : at + LANES, at:] = gram_block(held, at)
    for s in range(early, streams):
        for copy in flying[s]:
            copy.wait()
    held = rows_all[early:].reshape(-1, rank)
    device, _ = other
    copies = []
    for i, at in enumerate(range(0, rank, LANES)):
        late = gram_block(held, at)
        gram_own[at : at + LANES, at:] = gram_own[at : at + LANES, at:] + late if early else late
        copy = pltpu.make_async_remote_copy(
            src_ref=gram_own.at[pl.ds(at, LANES), pl.ds(at, rank - at)],
            dst_ref=gram_in.at[pl.ds(at, LANES), pl.ds(at, rank - at)],
            send_sem=gram_send.at[i],
            recv_sem=gram_recv.at[i],
            device_id=device,
            device_id_type=MESH,
        )
        copy.start()
        copies.append(copy)
    for number in range(n_narrow):
        for s in range(streams):
            at = (number * streams + s) * rows
            owned_ref[at : at + rows, :] = rows_all[s, place_of(orders[s], w * n_narrow + number)]
    for at, copy in zip(range(0, rank, LANES), copies):
        copy.wait()
        place = (slice(at, at + LANES), slice(at, rank))
        gram_ref[place] = gram_own[place] + gram_in[place]
        if at > 0:
            gram_ref[at : at + LANES, :at] = jnp.zeros((LANES, at), jnp.float32)


def sum_and_gather(tile_values, tile_row, tile_col, basis, n_wide, n_narrow):
    count, edge, _ = tile_values.shape
    held_rows, rank = basis.shape
    total_rows = COLS_DEV * n_wide
    devices = n_wide * n_narrow
    chunk = total_rows // devices
    orders = stream_orders(n_wide, n_narrow, chunk)
    steps, streams = len(orders[0]), len(orders)
    rows = chunk // streams
    recvs, accs = [], []
    for order in orders:
        recv, acc = [], []
        for step in range(1, steps):
            up, size, down = split_sizes(order, step)
            recv.append(pltpu.VMEM((size - 1, up, down, rows, rank), jnp.float32))
            acc.append(pltpu.VMEM((up, size, down, rows, rank), jnp.float32))
        recvs.append(recv)
        accs.append(acc)
    up, size, down = split_sizes(orders[0], 0)
    col_blocks = total_rows // edge
    strip = edge // HALVES
    up = up // (col_blocks * HALVES)
    most = max(2 ** len(group) for group in orders[0]) - 1
    dma = pltpu.SemaphoreType.DMA
    sems = [dma((1,)), dma((HALVES, count))] + [dma((col_blocks, HALVES))] * 2
    sems += [dma((steps, streams, most))] * 4 + [dma((rank // LANES,))] * 2
    square = pltpu.VMEM((rank, rank), jnp.float32)
    return pl.pallas_call(
        functools.partial(sum_gather_kernel, n_narrow, orders),
        out_shape=[
            jax.ShapeDtypeStruct((rank, rank), jnp.float32),
            jax.ShapeDtypeStruct((chunk * n_narrow, rank), jnp.float32),
        ],
        in_specs=[pl.BlockSpec(memory_space=pltpu.SMEM)] * 2 + [pl.BlockSpec(memory_space=pl.ANY)] * 2,
        out_specs=[pl.BlockSpec(memory_space=pltpu.VMEM)] * 2,
        scratch_shapes=[
            pltpu.VMEM((HALVES, count, edge, strip), jnp.bfloat16),
            pltpu.VMEM((held_rows, rank), jnp.float32),
            pltpu.VMEM((held_rows // edge, edge, rank), jnp.bfloat16),
            pltpu.VMEM((col_blocks, HALVES, up, size, down, chunk, rank), jnp.float32),
            pltpu.VMEM((col_blocks, HALVES, up, down, chunk, rank), jnp.float32),
            recvs,
            accs,
            pltpu.VMEM((streams, devices // 2, rows, rank), jnp.float32),
            square,
            square,
            sems,
        ],
        compiler_params=pltpu.CompilerParams(collective_id=0, has_side_effects=True, vmem_limit_bytes=VMEM_LIMIT),
    )(tile_row, tile_col, tile_values, basis)


PANEL = 8
OUTER = 32


def splat(value):
    return jnp.broadcast_to(value, (PANEL, LANES))


def finish_kernel(total_rows, gram_ref, owned_ref, out_ref, work):
    owned, rank = owned_ref.shape
    width = work.shape[1]
    work[:, :rank] = gram_ref[...] * (1.0 / total_rows)
    filled = jnp.concatenate([owned_ref[...], jnp.zeros((width - rank - owned, rank), jnp.float32)], axis=0)
    work[:, rank:] = filled.T

    for outer in range(0, rank, OUTER):
        base = (outer // LANES) * LANES
        blocks = list(range(base, width, LANES))
        groups = [
            [work[outer + g : outer + g + PANEL, c : c + LANES] for c in blocks] for g in range(0, OUTER, PANEL)
        ]
        for p in range(OUTER // PANEL):
            k = outer + p * PANEL - base
            head = groups[p][0]
            cols = [splat(head[:, k + j : k + j + 1]) for j in range(PANEL)]
            entry = [[splat(cols[j][i : i + 1, :]) for j in range(i + 1)] for i in range(PANEL)]
            scale = []
            for j in range(PANEL):
                scale.append(lax.rsqrt(entry[j][j]))
                for i in range(j + 1, PANEL):
                    entry[i][j] = entry[i][j] * scale[j]
                for i in range(j + 1, PANEL):
                    for m in range(j + 1, i + 1):
                        entry[i][m] = entry[i][m] - entry[i][j] * entry[m][j]
            solved = [[splat(block[j : j + 1, :]) for block in groups[p]] for j in range(PANEL)]
            for j in range(PANEL):
                solved[j] = [v * scale[j] for v in solved[j]]
                for i in range(j + 1, PANEL):
                    solved[i] = [a - entry[i][j] * v for a, v in zip(solved[i], solved[j])]
            place = lax.broadcasted_iota(jnp.int32, (PANEL, LANES), 0)
            final = solved[0]
            for j in range(1, PANEL):
                final = [jnp.where(place == j, v, f) for v, f in zip(solved[j], final)]
            for g in range(p + 1, OUTER // PANEL):
                low = groups[g][0]
                mult = [splat(low[:, k + j : k + j + 1]) for j in range(PANEL)]
                for j in range(PANEL):
                    mult[j] = mult[j] * scale[j]
                    for i in range(j + 1, PANEL):
                        mult[i] = mult[i] - entry[i][j] * mult[j]
                for j in range(PANEL):
                    groups[g] = [a - mult[j] * v for a, v in zip(groups[g], solved[j])]
            row = outer + p * PANEL
            for c, f in zip(blocks, final):
                work[row : row + PANEL, c : c + LANES] = f
        after = outer + OUTER
        if after < rank:
            start = (after // LANES) * LANES
            done = work[outer:after, start:]
            update = lax.dot_general(
                done[:, after - start : rank - start],
                done,
                (((0,), (0,)), ((), ())),
                precision=HIGHEST,
                preferred_element_type=jnp.float32,
            )
            work[after:rank, start:] -= update
    out_ref[...] = work[:, rank:].T[:owned]


def finish(gram, owned_rows, total_rows):
    owned, rank = owned_rows.shape
    width = rank + -(-owned // LANES) * LANES
    block = pl.BlockSpec(memory_space=pltpu.VMEM)
    return pl.pallas_call(
        functools.partial(finish_kernel, total_rows),
        out_shape=jax.ShapeDtypeStruct((owned, rank), jnp.float32),
        in_specs=[block] * 2,
        out_specs=block,
        scratch_shapes=[pltpu.VMEM((rank, width), jnp.float32)],
        compiler_params=pltpu.CompilerParams(vmem_limit_bytes=FINISH_LIMIT),
    )(gram, owned_rows)


def solution(mesh):
    n_wide, n_narrow = mesh.shape["wide"], mesh.shape["narrow"]

    def body(tile_values, tile_row, tile_col, basis):
        gram, owned_rows = sum_and_gather(tile_values, tile_row, tile_col, basis, n_wide, n_narrow)
        return finish(gram, owned_rows, COLS_DEV * n_wide)

    in_specs = (
        P(("wide", "narrow"), None, None),
        P(("wide", "narrow")),
        P(("wide", "narrow")),
        P(("wide", "narrow"), None),
    )
    return jax.shard_map(body, mesh=mesh, in_specs=in_specs, out_specs=P("wide", None), check_vma=False)
```

```python
import functools

import jax
import jax.numpy as jnp
from jax import lax
from jax.experimental import pallas as pl
from jax.experimental.pallas import tpu as pltpu
from jax.sharding import PartitionSpec as P

MESH = pl.DeviceIdType.MESH
HIGHEST = lax.Precision.HIGHEST
VMEM_LIMIT = 62 * 1024 * 1024
FINISH_LIMIT = 62 * 1024 * 1024
HALVES = 2
COLS_DEV = 64
LANES = 128


def stream_orders(n_wide, n_narrow, chunk_rows):
    nb = n_narrow.bit_length() - 1
    wb = n_wide.bit_length() - 1
    core = [(nb,)]
    narrow = [(i,) for i in range(nb)]
    second = [(nb + i,) for i in range(1, min(wb, 2))]
    rest = [tuple(range(nb + i, min(nb + i + 2, nb + wb))) for i in range(2, wb, 2)]
    pair = [core + narrow + second + rest, core + second + narrow + rest]
    if chunk_rows % 32 == 0:
        return pair + pair
    return pair if chunk_rows % 16 == 0 else pair[:1]


def split_sizes(order, step):
    left = sorted(b for group in order[step:] for b in group)
    at = left.index(order[step][0])
    size = len(order[step])
    return 2 ** (len(left) - at - size), 2**size, 2**at


def place_of(order, number):
    place, scale = 0, 1
    for group in reversed(order[1:]):
        place = place + ((number // 2 ** group[0]) % 2 ** len(group)) * scale
        scale = scale * 2 ** len(group)
    return place


def sum_gather_kernel(n_narrow, orders, row_ref, col_ref, tile_hbm, basis_hbm, gram_ref, owned_ref, *scratch):
    tiles, basis, rounded, part, recv0, recvs, accs, rows_all, gram_own, gram_in, sems = scratch
    w, n = lax.axis_index("wide"), lax.axis_index("narrow")
    me = w * n_narrow + n
    steps, streams = len(orders[0]), len(orders)
    rows, rank = rows_all.shape[2], rows_all.shape[3]
    basis_sem, tile_sem, core_send, core_recv, send_sem, recv_sem, gather_send, gather_recv, gram_send, gram_recv = sems
    count, edge, strip = tiles.shape[1:]

    def partner(group, delta):
        other, digit = me, (me // 2 ** group[0]) % 2 ** len(group)
        for i, b in enumerate(group):
            if (delta >> i) & 1:
                turn = 1 - 2 * ((me // 2**b) % 2)
                other, digit = other + turn * 2**b, digit + turn * 2**i
        return {"wide": other // n_narrow, "narrow": other % n_narrow}, digit

    barrier = pltpu.get_barrier_semaphore()
    met = 0
    for group in orders[0]:
        for delta in range(1, 2 ** len(group)):
            device, _ = partner(group, delta)
            pl.semaphore_signal(barrier, inc=1, device_id=device, device_id_type=MESH)
            met += 1

    def block_of(step, s, digit):
        if step == 0:
            return part.at[:, :, :, digit, :, pl.ds(s * rows, rows)]
        return accs[s][step - 1].at[:, digit]

    def start_sum(step, s):
        group, copies = orders[s][step], []
        for delta in range(1, 2 ** len(group)):
            device, digit = partner(group, delta)
            copy = pltpu.make_async_remote_copy(
                src_ref=block_of(step, s, digit),
                dst_ref=recvs[s][step - 1].at[delta - 1],
                send_sem=send_sem.at[step, s, delta - 1],
                recv_sem=recv_sem.at[step, s, delta - 1],
                device_id=device,
                device_id_type=MESH,
            )
            copy.start()
            copies.append(copy)
        return copies

    def start_gather(step, s):
        group, copies = orders[s][step], []
        size = 1
        for later in orders[s][step + 1 :]:
            size = size * 2 ** len(later)
        place = place_of(orders[s], me)
        block = rows_all.at[s, pl.ds((place // size) * size, size)]
        for delta in range(1, 2 ** len(group)):
            device, _ = partner(group, delta)
            copy = pltpu.make_async_remote_copy(
                src_ref=block,
                dst_ref=block,
                send_sem=gather_send.at[step, s, delta - 1],
                recv_sem=gather_recv.at[step, s, delta - 1],
                device_id=device,
                device_id_type=MESH,
            )
            copy.start()
            copies.append(copy)
        return copies

    copies = [pltpu.make_async_copy(basis_hbm, basis, basis_sem.at[0])]
    for h in range(HALVES):
        for t in range(count):
            source = tile_hbm.at[t, :, pl.ds(h * strip, strip)]
            copies.append(pltpu.make_async_copy(source, tiles.at[h, t], tile_sem.at[h, t]))
    for copy in copies:
        copy.start()
    copies[0].wait()
    rounded[...] = basis[...].astype(jnp.bfloat16).reshape(rounded.shape)
    core, other = (me // 2 ** orders[0][0][0]) % 2, partner(orders[0][0], 1)
    core_copies = []
    for h in range(HALVES):
        for t in range(count):
            copies[1 + h * count + t].wait()
            product = lax.dot_general(
                tiles[h, t], rounded[row_ref[t]], (((0,), (0,)), ((), ())), preferred_element_type=jnp.float32
            ).reshape(part.shape[2:])
            for c in range(part.shape[0]):
                term = jnp.where(col_ref[t] == c, product, 0.0)
                part[c, h] = term if t == 0 else part[c, h] + term
        if h == 0:
            pl.semaphore_wait(barrier, met)
        for c in range(part.shape[0]):
            copy = pltpu.make_async_remote_copy(
                src_ref=part.at[c, h, :, other[1]],
                dst_ref=recv0.at[c, h],
                send_sem=core_send.at[c, h],
                recv_sem=core_recv.at[c, h],
                device_id=other[0],
                device_id_type=MESH,
            )
            copy.start()
            core_copies.append(copy)
    for copy in core_copies:
        copy.wait()
    flying = []
    for s in range(streams):
        total = block_of(0, s, core)[...] + recv0[:, :, :, :, s * rows : (s + 1) * rows]
        accs[s][0][...] = total.reshape(accs[s][0].shape)
        flying.append(start_sum(1, s))

    for step in range(1, steps):
        for s in range(streams):
            group = orders[s][step]
            digit = (me // 2 ** group[0]) % 2 ** len(group)
            total = block_of(step, s, digit)[...]
            for delta, copy in enumerate(flying[s]):
                copy.wait()
                total = total + recvs[s][step - 1][delta]
            if step < steps - 1:
                accs[s][step][...] = total.reshape(accs[s][step].shape)
                flying[s] = start_sum(step + 1, s)
            else:
                rows_all[s, pl.ds(place_of(orders[s], me), 1)] = total.reshape((1, rows, rank))
                flying[s] = start_gather(step, s)
    for step in range(steps - 1, 1, -1):
        for s in range(streams):
            for copy in flying[s]:
                copy.wait()
            flying[s] = start_gather(step - 1, s)

    def gram_block(held, at):
        return lax.dot_general(
            held[:, at : at + LANES],
            held[:, at:],
            (((0,), (0,)), ((), ())),
            precision=HIGHEST,
            preferred_element_type=jnp.float32,
        )

    early = streams // 2
    for s in range(early):
        for copy in flying[s]:
            copy.wait()
    if early:
        held = rows_all[:early].reshape(-1, rank)
        for at in range(0, rank, LANES):
            gram_own[at : at + LANES, at:] = gram_block(held, at)
    for s in range(early, streams):
        for copy in flying[s]:
            copy.wait()
    held = rows_all[early:].reshape(-1, rank)
    device, _ = other
    copies = []
    for i, at in enumerate(range(0, rank, LANES)):
        late = gram_block(held, at)
        gram_own[at : at + LANES, at:] = gram_own[at : at + LANES, at:] + late if early else late
        copy = pltpu.make_async_remote_copy(
            src_ref=gram_own.at[pl.ds(at, LANES), pl.ds(at, rank - at)],
            dst_ref=gram_in.at[pl.ds(at, LANES), pl.ds(at, rank - at)],
            send_sem=gram_send.at[i],
            recv_sem=gram_recv.at[i],
            device_id=device,
            device_id_type=MESH,
        )
        copy.start()
        copies.append(copy)
    for number in range(n_narrow):
        for s in range(streams):
            at = (number * streams + s) * rows
            owned_ref[at : at + rows, :] = rows_all[s, place_of(orders[s], w * n_narrow + number)]
    for at, copy in zip(range(0, rank, LANES), copies):
        copy.wait()
        place = (slice(at, at + LANES), slice(at, rank))
        gram_ref[place] = gram_own[place] + gram_in[place]
        if at > 0:
            gram_ref[at : at + LANES, :at] = jnp.zeros((LANES, at), jnp.float32)


def sum_and_gather(tile_values, tile_row, tile_col, basis, n_wide, n_narrow):
    count, edge, _ = tile_values.shape
    held_rows, rank = basis.shape
    total_rows = COLS_DEV * n_wide
    devices = n_wide * n_narrow
    chunk = total_rows // devices
    orders = stream_orders(n_wide, n_narrow, chunk)
    steps, streams = len(orders[0]), len(orders)
    rows = chunk // streams
    recvs, accs = [], []
    for order in orders:
        recv, acc = [], []
        for step in range(1, steps):
            up, size, down = split_sizes(order, step)
            recv.append(pltpu.VMEM((size - 1, up, down, rows, rank), jnp.float32))
            acc.append(pltpu.VMEM((up, size, down, rows, rank), jnp.float32))
        recvs.append(recv)
        accs.append(acc)
    up, size, down = split_sizes(orders[0], 0)
    col_blocks = total_rows // edge
    strip = edge // HALVES
    up = up // (col_blocks * HALVES)
    most = max(2 ** len(group) for group in orders[0]) - 1
    dma = pltpu.SemaphoreType.DMA
    sems = [dma((1,)), dma((HALVES, count))] + [dma((col_blocks, HALVES))] * 2
    sems += [dma((steps, streams, most))] * 4 + [dma((rank // LANES,))] * 2
    square = pltpu.VMEM((rank, rank), jnp.float32)
    return pl.pallas_call(
        functools.partial(sum_gather_kernel, n_narrow, orders),
        out_shape=[
            jax.ShapeDtypeStruct((rank, rank), jnp.float32),
            jax.ShapeDtypeStruct((chunk * n_narrow, rank), jnp.float32),
        ],
        in_specs=[pl.BlockSpec(memory_space=pltpu.SMEM)] * 2 + [pl.BlockSpec(memory_space=pl.ANY)] * 2,
        out_specs=[pl.BlockSpec(memory_space=pltpu.VMEM)] * 2,
        scratch_shapes=[
            pltpu.VMEM((HALVES, count, edge, strip), jnp.bfloat16),
            pltpu.VMEM((held_rows, rank), jnp.float32),
            pltpu.VMEM((held_rows // edge, edge, rank), jnp.bfloat16),
            pltpu.VMEM((col_blocks, HALVES, up, size, down, chunk, rank), jnp.float32),
            pltpu.VMEM((col_blocks, HALVES, up, down, chunk, rank), jnp.float32),
            recvs,
            accs,
            pltpu.VMEM((streams, devices // 2, rows, rank), jnp.float32),
            square,
            square,
            sems,
        ],
        compiler_params=pltpu.CompilerParams(collective_id=0, has_side_effects=True, vmem_limit_bytes=VMEM_LIMIT),
    )(tile_row, tile_col, tile_values, basis)


PANEL = 8
OUTER = 64


def splat(value):
    return jnp.broadcast_to(value, (PANEL, LANES))


def finish_kernel(total_rows, gram_ref, owned_ref, out_ref, work):
    owned, rank = owned_ref.shape
    width = work.shape[1]
    gram = gram_ref[...] * (1.0 / total_rows)
    row = lax.broadcasted_iota(jnp.int32, gram.shape, 0)
    diagonal = jnp.where(row == lax.broadcasted_iota(jnp.int32, gram.shape, 1), gram, 0.0)
    across = lax.rsqrt(jnp.sum(diagonal, axis=0, keepdims=True))
    down = lax.rsqrt(jnp.sum(diagonal, axis=1, keepdims=True))
    work[:, :rank] = gram * across * down
    filled = jnp.concatenate(
        [owned_ref[...] * across, jnp.zeros((width - rank - owned, rank), jnp.float32)], axis=0
    )
    work[:, rank:] = filled.T

    for outer in range(0, rank, OUTER):
        base = (outer // LANES) * LANES
        blocks = list(range(base, width, LANES))
        groups = [
            [work[outer + g : outer + g + PANEL, c : c + LANES] for c in blocks] for g in range(0, OUTER, PANEL)
        ]
        for p in range(OUTER // PANEL):
            k = outer + p * PANEL - base
            head = groups[p][0]
            cols = [splat(head[:, k + j : k + j + 1]) for j in range(PANEL)]
            entry = [[splat(cols[j][i : i + 1, :]) for j in range(i + 1)] for i in range(PANEL)]
            scale = []
            for j in range(0, PANEL, 2):
                a, b, c = entry[j][j], entry[j + 1][j], entry[j + 1][j + 1]
                first = lax.rsqrt(a)
                second = first * lax.rsqrt(a * c - b * b)
                scale += [first, a * second]
                for i in range(j + 2, PANEL):
                    x, y = entry[i][j], entry[i][j + 1]
                    entry[i][j], entry[i][j + 1] = x * first, (y * a - x * b) * second
                entry[j + 1][j] = b * first
                for i in range(j + 2, PANEL):
                    for m in range(j + 2, i + 1):
                        drop = entry[i][j] * entry[m][j] + entry[i][j + 1] * entry[m][j + 1]
                        entry[i][m] = entry[i][m] - drop
            solved = [[splat(block[j : j + 1, :]) for block in groups[p]] for j in range(PANEL)]
            for j in range(PANEL):
                solved[j] = [v * scale[j] for v in solved[j]]
                for i in range(j + 1, PANEL):
                    solved[i] = [a - entry[i][j] * v for a, v in zip(solved[i], solved[j])]
            place = lax.broadcasted_iota(jnp.int32, (PANEL, LANES), 0)
            final = solved[0]
            for j in range(1, PANEL):
                final = [jnp.where(place == j, v, f) for v, f in zip(solved[j], final)]
            for g in range(p + 1, OUTER // PANEL):
                low = groups[g][0]
                mult = [splat(low[:, k + j : k + j + 1]) for j in range(PANEL)]
                for j in range(PANEL):
                    mult[j] = mult[j] * scale[j]
                    for i in range(j + 1, PANEL):
                        mult[i] = mult[i] - entry[i][j] * mult[j]
                for j in range(PANEL):
                    groups[g] = [a - mult[j] * v for a, v in zip(groups[g], solved[j])]
            row = outer + p * PANEL
            for c, f in zip(blocks, final):
                work[row : row + PANEL, c : c + LANES] = f
        after = outer + OUTER
        if after < rank:
            start = (after // LANES) * LANES
            done = work[outer:after, start:]
            update = lax.dot_general(
                done[:, after - start : rank - start],
                done,
                (((0,), (0,)), ((), ())),
                precision=HIGHEST,
                preferred_element_type=jnp.float32,
            )
            work[after:rank, start:] -= update
    out_ref[...] = work[:, rank:].T[:owned]


def finish(gram, owned_rows, total_rows):
    owned, rank = owned_rows.shape
    width = rank + -(-owned // LANES) * LANES
    block = pl.BlockSpec(memory_space=pltpu.VMEM)
    return pl.pallas_call(
        functools.partial(finish_kernel, total_rows),
        out_shape=jax.ShapeDtypeStruct((owned, rank), jnp.float32),
        in_specs=[block] * 2,
        out_specs=block,
        scratch_shapes=[pltpu.VMEM((rank, width), jnp.float32)],
        compiler_params=pltpu.CompilerParams(vmem_limit_bytes=FINISH_LIMIT),
    )(gram, owned_rows)


def solution(mesh):
    n_wide, n_narrow = mesh.shape["wide"], mesh.shape["narrow"]

    def body(tile_values, tile_row, tile_col, basis):
        gram, owned_rows = sum_and_gather(tile_values, tile_row, tile_col, basis, n_wide, n_narrow)
        return finish(gram, owned_rows, COLS_DEV * n_wide)

    in_specs = (
        P(("wide", "narrow"), None, None),
        P(("wide", "narrow")),
        P(("wide", "narrow")),
        P(("wide", "narrow"), None),
    )
    return jax.shard_map(body, mesh=mesh, in_specs=in_specs, out_specs=P("wide", None), check_vma=False)
```

```python
import functools

import jax
import jax.numpy as jnp
from jax import lax
from jax.experimental import pallas as pl
from jax.experimental.pallas import tpu as pltpu
from jax.sharding import PartitionSpec as P

MESH = pl.DeviceIdType.MESH
HIGHEST = lax.Precision.HIGHEST
VMEM_LIMIT = 62 * 1024 * 1024
FINISH_LIMIT = 62 * 1024 * 1024
HALVES = 2
COLS_DEV = 64
LANES = 128


def stream_orders(n_wide, n_narrow, chunk_rows):
    nb = n_narrow.bit_length() - 1
    wb = n_wide.bit_length() - 1
    core = [(nb,)]
    plane = [tuple(range(max(nb - 1, 0), nb)) + tuple(range(nb + 1, nb + min(wb, 2)))]
    narrow = [(i,) for i in range(nb - 1)]
    rest = [tuple(range(nb + i, min(nb + i + 2, nb + wb))) for i in range(2, wb, 2)]
    order = core + plane + narrow + rest
    return [order] * (4 if chunk_rows % 32 == 0 else 2 if chunk_rows % 16 == 0 else 1)


def digit_of(number, group):
    return sum(((number // 2**b) % 2) * 2**i for i, b in enumerate(group))


def split_sizes(order, step):
    left = sorted(b for group in order[step:] for b in group)
    at = left.index(order[step][0])
    size = len(order[step])
    return 2 ** (len(left) - at - size), 2**size, 2**at


def place_of(order, number):
    place, scale = 0, 1
    for group in reversed(order[1:]):
        place = place + digit_of(number, group) * scale
        scale = scale * 2 ** len(group)
    return place


def sum_gather_kernel(n_narrow, orders, row_ref, col_ref, tile_hbm, basis_hbm, gram_ref, owned_ref, *scratch):
    tiles, basis, rounded, part, recv0, recvs, accs, rows_all, gram_own, gram_in, sems = scratch
    w, n = lax.axis_index("wide"), lax.axis_index("narrow")
    me = w * n_narrow + n
    steps, streams = len(orders[0]), len(orders)
    rows, rank = rows_all.shape[2], rows_all.shape[3]
    basis_sem, tile_sem, core_send, core_recv, send_sem, recv_sem, gather_send, gather_recv, gram_send, gram_recv = sems
    count, edge, strip = tiles.shape[1:]

    def partner(group, delta):
        other, digit = me, digit_of(me, group)
        for i, b in enumerate(group):
            if (delta >> i) & 1:
                turn = 1 - 2 * ((me // 2**b) % 2)
                other, digit = other + turn * 2**b, digit + turn * 2**i
        return {"wide": other // n_narrow, "narrow": other % n_narrow}, digit

    barrier = pltpu.get_barrier_semaphore()
    met = 0
    for group in orders[0]:
        for delta in range(1, 2 ** len(group)):
            device, _ = partner(group, delta)
            pl.semaphore_signal(barrier, inc=1, device_id=device, device_id_type=MESH)
            met += 1

    def block_of(step, s, digit):
        if step == 0:
            return part.at[:, :, :, digit, :, pl.ds(s * rows, rows)]
        return accs[s][step - 1].at[:, digit]

    def start_sum(step, s):
        group, copies = orders[s][step], []
        for delta in range(1, 2 ** len(group)):
            device, digit = partner(group, delta)
            copy = pltpu.make_async_remote_copy(
                src_ref=block_of(step, s, digit),
                dst_ref=recvs[s][step - 1].at[delta - 1],
                send_sem=send_sem.at[step, s, delta - 1],
                recv_sem=recv_sem.at[step, s, delta - 1],
                device_id=device,
                device_id_type=MESH,
            )
            copy.start()
            copies.append(copy)
        return copies

    def start_gather(step, s):
        group, copies = orders[s][step], []
        size = 1
        for later in orders[s][step + 1 :]:
            size = size * 2 ** len(later)
        place = place_of(orders[s], me)
        block = rows_all.at[s, pl.ds((place // size) * size, size)]
        for delta in range(1, 2 ** len(group)):
            device, _ = partner(group, delta)
            copy = pltpu.make_async_remote_copy(
                src_ref=block,
                dst_ref=block,
                send_sem=gather_send.at[step, s, delta - 1],
                recv_sem=gather_recv.at[step, s, delta - 1],
                device_id=device,
                device_id_type=MESH,
            )
            copy.start()
            copies.append(copy)
        return copies

    copies = [pltpu.make_async_copy(basis_hbm, basis, basis_sem.at[0])]
    for h in range(HALVES):
        for t in range(count):
            source = tile_hbm.at[t, :, pl.ds(h * strip, strip)]
            copies.append(pltpu.make_async_copy(source, tiles.at[h, t], tile_sem.at[h, t]))
    for copy in copies:
        copy.start()
    copies[0].wait()
    rounded[...] = basis[...].astype(jnp.bfloat16).reshape(rounded.shape)
    core, other = digit_of(me, orders[0][0]), partner(orders[0][0], 1)
    core_copies = []
    for h in range(HALVES):
        for t in range(count):
            copies[1 + h * count + t].wait()
            product = lax.dot_general(
                tiles[h, t], rounded[row_ref[t]], (((0,), (0,)), ((), ())), preferred_element_type=jnp.float32
            ).reshape(part.shape[2:])
            for c in range(part.shape[0]):
                term = jnp.where(col_ref[t] == c, product, 0.0)
                part[c, h] = term if t == 0 else part[c, h] + term
        if h == 0:
            pl.semaphore_wait(barrier, met)
        for c in range(part.shape[0]):
            copy = pltpu.make_async_remote_copy(
                src_ref=part.at[c, h, :, other[1]],
                dst_ref=recv0.at[c, h],
                send_sem=core_send.at[c, h],
                recv_sem=core_recv.at[c, h],
                device_id=other[0],
                device_id_type=MESH,
            )
            copy.start()
            core_copies.append(copy)
    for copy in core_copies:
        copy.wait()
    flying = []
    for s in range(streams):
        total = block_of(0, s, core)[...] + recv0[:, :, :, :, s * rows : (s + 1) * rows]
        accs[s][0][...] = total.reshape(accs[s][0].shape)
        flying.append(start_sum(1, s))

    for step in range(1, steps):
        for s in range(streams):
            group = orders[s][step]
            digit = digit_of(me, group)
            total = block_of(step, s, digit)[...]
            for delta, copy in enumerate(flying[s]):
                copy.wait()
                total = total + recvs[s][step - 1][delta]
            if step < steps - 1:
                accs[s][step][...] = total.reshape(accs[s][step].shape)
                flying[s] = start_sum(step + 1, s)
            else:
                rows_all[s, pl.ds(place_of(orders[s], me), 1)] = total.reshape((1, rows, rank))
                flying[s] = start_gather(step, s)
    for step in range(steps - 1, 1, -1):
        for s in range(streams):
            for copy in flying[s]:
                copy.wait()
            flying[s] = start_gather(step - 1, s)

    def gram_block(held, at):
        return lax.dot_general(
            held[:, at : at + LANES],
            held[:, at:],
            (((0,), (0,)), ((), ())),
            precision=HIGHEST,
            preferred_element_type=jnp.float32,
        )

    early = streams // 2
    for s in range(early):
        for copy in flying[s]:
            copy.wait()
    if early:
        held = rows_all[:early].reshape(-1, rank)
        for at in range(0, rank, LANES):
            gram_own[at : at + LANES, at:] = gram_block(held, at)
    for s in range(early, streams):
        for copy in flying[s]:
            copy.wait()
    held = rows_all[early:].reshape(-1, rank)
    device, _ = other
    copies = []
    for i, at in enumerate(range(0, rank, LANES)):
        late = gram_block(held, at)
        gram_own[at : at + LANES, at:] = gram_own[at : at + LANES, at:] + late if early else late
        copy = pltpu.make_async_remote_copy(
            src_ref=gram_own.at[pl.ds(at, LANES), pl.ds(at, rank - at)],
            dst_ref=gram_in.at[pl.ds(at, LANES), pl.ds(at, rank - at)],
            send_sem=gram_send.at[i],
            recv_sem=gram_recv.at[i],
            device_id=device,
            device_id_type=MESH,
        )
        copy.start()
        copies.append(copy)
    for number in range(n_narrow):
        for s in range(streams):
            at = (number * streams + s) * rows
            owned_ref[at : at + rows, :] = rows_all[s, place_of(orders[s], w * n_narrow + number)]
    for at, copy in zip(range(0, rank, LANES), copies):
        copy.wait()
        place = (slice(at, at + LANES), slice(at, rank))
        gram_ref[place] = gram_own[place] + gram_in[place]
        if at > 0:
            gram_ref[at : at + LANES, :at] = jnp.zeros((LANES, at), jnp.float32)


def sum_and_gather(tile_values, tile_row, tile_col, basis, n_wide, n_narrow):
    count, edge, _ = tile_values.shape
    held_rows, rank = basis.shape
    total_rows = COLS_DEV * n_wide
    devices = n_wide * n_narrow
    chunk = total_rows // devices
    orders = stream_orders(n_wide, n_narrow, chunk)
    steps, streams = len(orders[0]), len(orders)
    rows = chunk // streams
    recvs, accs = [], []
    for order in orders:
        recv, acc = [], []
        for step in range(1, steps):
            up, size, down = split_sizes(order, step)
            recv.append(pltpu.VMEM((size - 1, up, down, rows, rank), jnp.float32))
            acc.append(pltpu.VMEM((up, size, down, rows, rank), jnp.float32))
        recvs.append(recv)
        accs.append(acc)
    up, size, down = split_sizes(orders[0], 0)
    col_blocks = total_rows // edge
    strip = edge // HALVES
    up = up // (col_blocks * HALVES)
    most = max(2 ** len(group) for group in orders[0]) - 1
    dma = pltpu.SemaphoreType.DMA
    sems = [dma((1,)), dma((HALVES, count))] + [dma((col_blocks, HALVES))] * 2
    sems += [dma((steps, streams, most))] * 4 + [dma((rank // LANES,))] * 2
    square = pltpu.VMEM((rank, rank), jnp.float32)
    return pl.pallas_call(
        functools.partial(sum_gather_kernel, n_narrow, orders),
        out_shape=[
            jax.ShapeDtypeStruct((rank, rank), jnp.float32),
            jax.ShapeDtypeStruct((chunk * n_narrow, rank), jnp.float32),
        ],
        in_specs=[pl.BlockSpec(memory_space=pltpu.SMEM)] * 2 + [pl.BlockSpec(memory_space=pl.ANY)] * 2,
        out_specs=[pl.BlockSpec(memory_space=pltpu.VMEM)] * 2,
        scratch_shapes=[
            pltpu.VMEM((HALVES, count, edge, strip), jnp.bfloat16),
            pltpu.VMEM((held_rows, rank), jnp.float32),
            pltpu.VMEM((held_rows // edge, edge, rank), jnp.bfloat16),
            pltpu.VMEM((col_blocks, HALVES, up, size, down, chunk, rank), jnp.float32),
            pltpu.VMEM((col_blocks, HALVES, up, down, chunk, rank), jnp.float32),
            recvs,
            accs,
            pltpu.VMEM((streams, devices // 2, rows, rank), jnp.float32),
            square,
            square,
            sems,
        ],
        compiler_params=pltpu.CompilerParams(collective_id=0, has_side_effects=True, vmem_limit_bytes=VMEM_LIMIT),
    )(tile_row, tile_col, tile_values, basis)


PANEL = 8
OUTER = 64


def splat(value):
    return jnp.broadcast_to(value, (PANEL, LANES))


def finish_kernel(total_rows, gram_ref, owned_ref, out_ref, work):
    owned, rank = owned_ref.shape
    width = work.shape[1]
    gram = gram_ref[...] * (1.0 / total_rows)
    row = lax.broadcasted_iota(jnp.int32, gram.shape, 0)
    diagonal = jnp.where(row == lax.broadcasted_iota(jnp.int32, gram.shape, 1), gram, 0.0)
    across = lax.rsqrt(jnp.sum(diagonal, axis=0, keepdims=True))
    down = lax.rsqrt(jnp.sum(diagonal, axis=1, keepdims=True))
    work[:, :rank] = gram * across * down
    filled = jnp.concatenate(
        [owned_ref[...] * across, jnp.zeros((width - rank - owned, rank), jnp.float32)], axis=0
    )
    work[:, rank:] = filled.T

    for outer in range(0, rank, OUTER):
        base = (outer // LANES) * LANES
        blocks = list(range(base, width, LANES))
        groups = [
            [work[outer + g : outer + g + PANEL, c : c + LANES] for c in blocks] for g in range(0, OUTER, PANEL)
        ]
        for p in range(OUTER // PANEL):
            k = outer + p * PANEL - base
            head = groups[p][0]
            cols = [splat(head[:, k + j : k + j + 1]) for j in range(PANEL)]
            entry = [[splat(cols[j][i : i + 1, :]) for j in range(i + 1)] for i in range(PANEL)]
            scale = []
            for j in range(0, PANEL, 2):
                a, b, c = entry[j][j], entry[j + 1][j], entry[j + 1][j + 1]
                first = lax.rsqrt(a)
                second = first * lax.rsqrt(a * c - b * b)
                scale += [first, a * second]
                for i in range(j + 2, PANEL):
                    x, y = entry[i][j], entry[i][j + 1]
                    entry[i][j], entry[i][j + 1] = x * first, (y * a - x * b) * second
                entry[j + 1][j] = b * first
                for i in range(j + 2, PANEL):
                    for m in range(j + 2, i + 1):
                        drop = entry[i][j] * entry[m][j] + entry[i][j + 1] * entry[m][j + 1]
                        entry[i][m] = entry[i][m] - drop
            solved = [[splat(block[j : j + 1, :]) for block in groups[p]] for j in range(PANEL)]
            for j in range(PANEL):
                solved[j] = [v * scale[j] for v in solved[j]]
                for i in range(j + 1, PANEL):
                    solved[i] = [a - entry[i][j] * v for a, v in zip(solved[i], solved[j])]
            place = lax.broadcasted_iota(jnp.int32, (PANEL, LANES), 0)
            final = solved[0]
            for j in range(1, PANEL):
                final = [jnp.where(place == j, v, f) for v, f in zip(solved[j], final)]
            for g in range(p + 1, OUTER // PANEL):
                low = groups[g][0]
                mult = [splat(low[:, k + j : k + j + 1]) for j in range(PANEL)]
                for j in range(PANEL):
                    mult[j] = mult[j] * scale[j]
                    for i in range(j + 1, PANEL):
                        mult[i] = mult[i] - entry[i][j] * mult[j]
                for j in range(PANEL):
                    groups[g] = [a - mult[j] * v for a, v in zip(groups[g], solved[j])]
            row = outer + p * PANEL
            for c, f in zip(blocks, final):
                work[row : row + PANEL, c : c + LANES] = f
        after = outer + OUTER
        if after < rank:
            start = (after // LANES) * LANES
            done = work[outer:after, start:]
            update = lax.dot_general(
                done[:, after - start : rank - start],
                done,
                (((0,), (0,)), ((), ())),
                precision=HIGHEST,
                preferred_element_type=jnp.float32,
            )
            work[after:rank, start:] -= update
    out_ref[...] = work[:, rank:].T[:owned]


def finish(gram, owned_rows, total_rows):
    owned, rank = owned_rows.shape
    width = rank + -(-owned // LANES) * LANES
    block = pl.BlockSpec(memory_space=pltpu.VMEM)
    return pl.pallas_call(
        functools.partial(finish_kernel, total_rows),
        out_shape=jax.ShapeDtypeStruct((owned, rank), jnp.float32),
        in_specs=[block] * 2,
        out_specs=block,
        scratch_shapes=[pltpu.VMEM((rank, width), jnp.float32)],
        compiler_params=pltpu.CompilerParams(vmem_limit_bytes=FINISH_LIMIT),
    )(gram, owned_rows)


def solution(mesh):
    n_wide, n_narrow = mesh.shape["wide"], mesh.shape["narrow"]

    def body(tile_values, tile_row, tile_col, basis):
        gram, owned_rows = sum_and_gather(tile_values, tile_row, tile_col, basis, n_wide, n_narrow)
        return finish(gram, owned_rows, COLS_DEV * n_wide)

    in_specs = (
        P(("wide", "narrow"), None, None),
        P(("wide", "narrow")),
        P(("wide", "narrow")),
        P(("wide", "narrow"), None),
    )
    return jax.shard_map(body, mesh=mesh, in_specs=in_specs, out_specs=P("wide", None), check_vma=False)
```

```python
import functools

import jax
import jax.numpy as jnp
from jax import lax
from jax.experimental import pallas as pl
from jax.experimental.pallas import tpu as pltpu
from jax.sharding import PartitionSpec as P

MESH = pl.DeviceIdType.MESH
HIGHEST = lax.Precision.HIGHEST
VMEM_LIMIT = 62 * 1024 * 1024
FINISH_LIMIT = 62 * 1024 * 1024
HALVES = 2
COLS_DEV = 64
LANES = 128


def stream_orders(n_wide, n_narrow, chunk_rows):
    nb = n_narrow.bit_length() - 1
    wb = n_wide.bit_length() - 1
    core = [(nb,)]
    plane = [tuple(range(max(nb - 1, 0), nb)) + tuple(range(nb + 1, nb + min(wb, 2)))]
    narrow = [(i,) for i in range(nb - 1)]
    rest = [tuple(range(nb + i, min(nb + i + 2, nb + wb))) for i in range(2, wb, 2)]
    order = core + plane + narrow + rest
    return [order] * (4 if chunk_rows % 32 == 0 else 2 if chunk_rows % 16 == 0 else 1)


def digit_of(number, group):
    return sum(((number // 2**b) % 2) * 2**i for i, b in enumerate(group))


def split_sizes(order, step):
    left = sorted(b for group in order[step:] for b in group)
    at = left.index(order[step][0])
    size = len(order[step])
    return 2 ** (len(left) - at - size), 2**size, 2**at


def place_of(order, number):
    place, scale = 0, 1
    for group in reversed(order[1:]):
        place = place + digit_of(number, group) * scale
        scale = scale * 2 ** len(group)
    return place


def sum_gather_kernel(n_narrow, orders, row_ref, col_ref, tile_hbm, basis_hbm, gram_ref, owned_ref, *scratch):
    tiles, basis, rounded, part, recv0, recvs, accs, rows_all, gram_own, gram_in, sems = scratch
    w, n = lax.axis_index("wide"), lax.axis_index("narrow")
    me = w * n_narrow + n
    steps, streams = len(orders[0]), len(orders)
    rows, rank = rows_all.shape[2], rows_all.shape[3]
    basis_sem, tile_sem, core_send, core_recv, send_sem, recv_sem, gather_send, gather_recv, gram_send, gram_recv = sems
    count, edge, strip = tiles.shape[1:]

    def partner(group, delta):
        other, digit = me, digit_of(me, group)
        for i, b in enumerate(group):
            if (delta >> i) & 1:
                turn = 1 - 2 * ((me // 2**b) % 2)
                other, digit = other + turn * 2**b, digit + turn * 2**i
        return {"wide": other // n_narrow, "narrow": other % n_narrow}, digit

    barrier = pltpu.get_barrier_semaphore()
    met = 0
    for group in orders[0]:
        for delta in range(1, 2 ** len(group)):
            device, _ = partner(group, delta)
            pl.semaphore_signal(barrier, inc=1, device_id=device, device_id_type=MESH)
            met += 1

    sent = []

    def block_of(step, s, digit):
        if step == 0:
            return part.at[:, :, :, digit, :, pl.ds(s * rows, rows)]
        return accs[s][step - 1].at[:, digit]

    def start_sum(step, s):
        group, copies = orders[s][step], []
        for delta in range(1, 2 ** len(group)):
            device, digit = partner(group, delta)
            copy = pltpu.make_async_remote_copy(
                src_ref=block_of(step, s, digit),
                dst_ref=recvs[s][step - 1].at[delta - 1],
                send_sem=send_sem.at[step, s, delta - 1],
                recv_sem=recv_sem.at[step, s, delta - 1],
                device_id=device,
                device_id_type=MESH,
            )
            copy.start()
            sent.append(copy)
            copies.append(copy)
        return copies

    def start_gather(step, s):
        group, copies = orders[s][step], []
        size = 1
        for later in orders[s][step + 1 :]:
            size = size * 2 ** len(later)
        place = place_of(orders[s], me)
        block = rows_all.at[s, pl.ds((place // size) * size, size)]
        for delta in range(1, 2 ** len(group)):
            device, _ = partner(group, delta)
            copy = pltpu.make_async_remote_copy(
                src_ref=block,
                dst_ref=block,
                send_sem=gather_send.at[step, s, delta - 1],
                recv_sem=gather_recv.at[step, s, delta - 1],
                device_id=device,
                device_id_type=MESH,
            )
            copy.start()
            sent.append(copy)
            copies.append(copy)
        return copies

    copies = [pltpu.make_async_copy(basis_hbm, basis, basis_sem.at[0])]
    for h in range(HALVES):
        for t in range(count):
            source = tile_hbm.at[t, :, pl.ds(h * strip, strip)]
            copies.append(pltpu.make_async_copy(source, tiles.at[h, t], tile_sem.at[h, t]))
    for copy in copies:
        copy.start()
    copies[0].wait()
    rounded[...] = basis[...].astype(jnp.bfloat16).reshape(rounded.shape)
    core, other = digit_of(me, orders[0][0]), partner(orders[0][0], 1)
    core_copies = []
    for h in range(HALVES):
        for t in range(count):
            copies[1 + h * count + t].wait()
            product = lax.dot_general(
                tiles[h, t], rounded[row_ref[t]], (((0,), (0,)), ((), ())), preferred_element_type=jnp.float32
            ).reshape(part.shape[2:])
            for c in range(part.shape[0]):
                term = jnp.where(col_ref[t] == c, product, 0.0)
                part[c, h] = term if t == 0 else part[c, h] + term
        if h == 0:
            pl.semaphore_wait(barrier, met)
        for c in range(part.shape[0]):
            copy = pltpu.make_async_remote_copy(
                src_ref=part.at[c, h, :, other[1]],
                dst_ref=recv0.at[c, h],
                send_sem=core_send.at[c, h],
                recv_sem=core_recv.at[c, h],
                device_id=other[0],
                device_id_type=MESH,
            )
            copy.start()
            sent.append(copy)
            core_copies.append(copy)
    for copy in core_copies:
        copy.wait_recv()
    flying = []
    for s in range(streams):
        total = block_of(0, s, core)[...] + recv0[:, :, :, :, s * rows : (s + 1) * rows]
        accs[s][0][...] = total.reshape(accs[s][0].shape)
        flying.append(start_sum(1, s))

    for step in range(1, steps):
        for s in range(streams):
            group = orders[s][step]
            digit = digit_of(me, group)
            total = block_of(step, s, digit)[...]
            for delta, copy in enumerate(flying[s]):
                copy.wait_recv()
                total = total + recvs[s][step - 1][delta]
            if step < steps - 1:
                accs[s][step][...] = total.reshape(accs[s][step].shape)
                flying[s] = start_sum(step + 1, s)
            else:
                rows_all[s, pl.ds(place_of(orders[s], me), 1)] = total.reshape((1, rows, rank))
                flying[s] = start_gather(step, s)
    for step in range(steps - 1, 1, -1):
        for s in range(streams):
            for copy in flying[s]:
                copy.wait_recv()
            flying[s] = start_gather(step - 1, s)

    def gram_block(held, at):
        return lax.dot_general(
            held[:, at : at + LANES],
            held[:, at:],
            (((0,), (0,)), ((), ())),
            precision=HIGHEST,
            preferred_element_type=jnp.float32,
        )

    early = streams // 2
    for s in range(early):
        for copy in flying[s]:
            copy.wait_recv()
    if early:
        held = rows_all[:early].reshape(-1, rank)
        for at in range(0, rank, LANES):
            gram_own[at : at + LANES, at:] = gram_block(held, at)
    for s in range(early, streams):
        for copy in flying[s]:
            copy.wait_recv()
    held = rows_all[early:].reshape(-1, rank)
    device, _ = other
    copies = []
    for i, at in enumerate(range(0, rank, LANES)):
        late = gram_block(held, at)
        gram_own[at : at + LANES, at:] = gram_own[at : at + LANES, at:] + late if early else late
        copy = pltpu.make_async_remote_copy(
            src_ref=gram_own.at[pl.ds(at, LANES), pl.ds(at, rank - at)],
            dst_ref=gram_in.at[pl.ds(at, LANES), pl.ds(at, rank - at)],
            send_sem=gram_send.at[i],
            recv_sem=gram_recv.at[i],
            device_id=device,
            device_id_type=MESH,
        )
        copy.start()
        sent.append(copy)
        copies.append(copy)
    for number in range(n_narrow):
        for s in range(streams):
            at = (number * streams + s) * rows
            owned_ref[at : at + rows, :] = rows_all[s, place_of(orders[s], w * n_narrow + number)]
    for at, copy in zip(range(0, rank, LANES), copies):
        copy.wait_recv()
        place = (slice(at, at + LANES), slice(at, rank))
        gram_ref[place] = gram_own[place] + gram_in[place]
        if at > 0:
            gram_ref[at : at + LANES, :at] = jnp.zeros((LANES, at), jnp.float32)
    for copy in sent:
        copy.wait_send()


def sum_and_gather(tile_values, tile_row, tile_col, basis, n_wide, n_narrow):
    count, edge, _ = tile_values.shape
    held_rows, rank = basis.shape
    total_rows = COLS_DEV * n_wide
    devices = n_wide * n_narrow
    chunk = total_rows // devices
    orders = stream_orders(n_wide, n_narrow, chunk)
    steps, streams = len(orders[0]), len(orders)
    rows = chunk // streams
    recvs, accs = [], []
    for order in orders:
        recv, acc = [], []
        for step in range(1, steps):
            up, size, down = split_sizes(order, step)
            recv.append(pltpu.VMEM((size - 1, up, down, rows, rank), jnp.float32))
            acc.append(pltpu.VMEM((up, size, down, rows, rank), jnp.float32))
        recvs.append(recv)
        accs.append(acc)
    up, size, down = split_sizes(orders[0], 0)
    col_blocks = total_rows // edge
    strip = edge // HALVES
    up = up // (col_blocks * HALVES)
    most = max(2 ** len(group) for group in orders[0]) - 1
    dma = pltpu.SemaphoreType.DMA
    sems = [dma((1,)), dma((HALVES, count))] + [dma((col_blocks, HALVES))] * 2
    sems += [dma((steps, streams, most))] * 4 + [dma((rank // LANES,))] * 2
    square = pltpu.VMEM((rank, rank), jnp.float32)
    return pl.pallas_call(
        functools.partial(sum_gather_kernel, n_narrow, orders),
        out_shape=[
            jax.ShapeDtypeStruct((rank, rank), jnp.float32),
            jax.ShapeDtypeStruct((chunk * n_narrow, rank), jnp.float32),
        ],
        in_specs=[pl.BlockSpec(memory_space=pltpu.SMEM)] * 2 + [pl.BlockSpec(memory_space=pl.ANY)] * 2,
        out_specs=[pl.BlockSpec(memory_space=pltpu.VMEM)] * 2,
        scratch_shapes=[
            pltpu.VMEM((HALVES, count, edge, strip), jnp.bfloat16),
            pltpu.VMEM((held_rows, rank), jnp.float32),
            pltpu.VMEM((held_rows // edge, edge, rank), jnp.bfloat16),
            pltpu.VMEM((col_blocks, HALVES, up, size, down, chunk, rank), jnp.float32),
            pltpu.VMEM((col_blocks, HALVES, up, down, chunk, rank), jnp.float32),
            recvs,
            accs,
            pltpu.VMEM((streams, devices // 2, rows, rank), jnp.float32),
            square,
            square,
            sems,
        ],
        compiler_params=pltpu.CompilerParams(collective_id=0, has_side_effects=True, vmem_limit_bytes=VMEM_LIMIT),
    )(tile_row, tile_col, tile_values, basis)


PANEL = 8
OUTER = 64


def splat(value):
    return jnp.broadcast_to(value, (PANEL, LANES))


def finish_kernel(total_rows, gram_ref, owned_ref, out_ref, work):
    owned, rank = owned_ref.shape
    width = work.shape[1]
    gram = gram_ref[...] * (1.0 / total_rows)
    row = lax.broadcasted_iota(jnp.int32, gram.shape, 0)
    diagonal = jnp.where(row == lax.broadcasted_iota(jnp.int32, gram.shape, 1), gram, 0.0)
    across = lax.rsqrt(jnp.sum(diagonal, axis=0, keepdims=True))
    down = lax.rsqrt(jnp.sum(diagonal, axis=1, keepdims=True))
    work[:, :rank] = gram * across * down
    filled = jnp.concatenate(
        [owned_ref[...] * across, jnp.zeros((width - rank - owned, rank), jnp.float32)], axis=0
    )
    work[:, rank:] = filled.T

    for outer in range(0, rank, OUTER):
        base = (outer // LANES) * LANES
        blocks = list(range(base, width, LANES))
        groups = [
            [work[outer + g : outer + g + PANEL, c : c + LANES] for c in blocks] for g in range(0, OUTER, PANEL)
        ]
        for p in range(OUTER // PANEL):
            k = outer + p * PANEL - base
            head = groups[p][0]
            cols = [splat(head[:, k + j : k + j + 1]) for j in range(PANEL)]
            entry = [[splat(cols[j][i : i + 1, :]) for j in range(i + 1)] for i in range(PANEL)]
            scale = []
            for j in range(0, PANEL, 2):
                a, b, c = entry[j][j], entry[j + 1][j], entry[j + 1][j + 1]
                first = lax.rsqrt(a)
                second = first * lax.rsqrt(a * c - b * b)
                scale += [first, a * second]
                for i in range(j + 2, PANEL):
                    x, y = entry[i][j], entry[i][j + 1]
                    entry[i][j], entry[i][j + 1] = x * first, (y * a - x * b) * second
                entry[j + 1][j] = b * first
                for i in range(j + 2, PANEL):
                    for m in range(j + 2, i + 1):
                        drop = entry[i][j] * entry[m][j] + entry[i][j + 1] * entry[m][j + 1]
                        entry[i][m] = entry[i][m] - drop
            solved = [[splat(block[j : j + 1, :]) for block in groups[p]] for j in range(PANEL)]
            for j in range(PANEL):
                solved[j] = [v * scale[j] for v in solved[j]]
                for i in range(j + 1, PANEL):
                    solved[i] = [a - entry[i][j] * v for a, v in zip(solved[i], solved[j])]
            place = lax.broadcasted_iota(jnp.int32, (PANEL, LANES), 0)
            final = solved[0]
            for j in range(1, PANEL):
                final = [jnp.where(place == j, v, f) for v, f in zip(solved[j], final)]
            for g in range(p + 1, OUTER // PANEL):
                low = groups[g][0]
                mult = [splat(low[:, k + j : k + j + 1]) for j in range(PANEL)]
                for j in range(PANEL):
                    mult[j] = mult[j] * scale[j]
                    for i in range(j + 1, PANEL):
                        mult[i] = mult[i] - entry[i][j] * mult[j]
                for j in range(PANEL):
                    groups[g] = [a - mult[j] * v for a, v in zip(groups[g], solved[j])]
            row = outer + p * PANEL
            for c, f in zip(blocks, final):
                work[row : row + PANEL, c : c + LANES] = f
        after = outer + OUTER
        if after < rank:
            start = (after // LANES) * LANES
            done = work[outer:after, start:]
            update = lax.dot_general(
                done[:, after - start : rank - start],
                done,
                (((0,), (0,)), ((), ())),
                precision=HIGHEST,
                preferred_element_type=jnp.float32,
            )
            work[after:rank, start:] -= update
    out_ref[...] = work[:, rank:].T[:owned]


def finish(gram, owned_rows, total_rows):
    owned, rank = owned_rows.shape
    width = rank + -(-owned // LANES) * LANES
    block = pl.BlockSpec(memory_space=pltpu.VMEM)
    return pl.pallas_call(
        functools.partial(finish_kernel, total_rows),
        out_shape=jax.ShapeDtypeStruct((owned, rank), jnp.float32),
        in_specs=[block] * 2,
        out_specs=block,
        scratch_shapes=[pltpu.VMEM((rank, width), jnp.float32)],
        compiler_params=pltpu.CompilerParams(vmem_limit_bytes=FINISH_LIMIT),
    )(gram, owned_rows)


def solution(mesh):
    n_wide, n_narrow = mesh.shape["wide"], mesh.shape["narrow"]

    def body(tile_values, tile_row, tile_col, basis):
        gram, owned_rows = sum_and_gather(tile_values, tile_row, tile_col, basis, n_wide, n_narrow)
        return finish(gram, owned_rows, COLS_DEV * n_wide)

    in_specs = (
        P(("wide", "narrow"), None, None),
        P(("wide", "narrow")),
        P(("wide", "narrow")),
        P(("wide", "narrow"), None),
    )
    return jax.shard_map(body, mesh=mesh, in_specs=in_specs, out_specs=P("wide", None), check_vma=False)
```
